256 devices in a mesh: row: 8 (over z), col: 32 (over y, x, core).
Axes of the slice: x: 4, y: 4, z: 8, core: 2. Of those that a mesh axis runs over, the one named last changes fastest.
Arguments:
- node_features: bfloat16 [32768, 256], P(('row', 'col')), may hold values from -6 to 6
- reorder_target: int32 [32768], P(('row', 'col')), may hold values from 0 to 4095, as said below
- weight_matrix: bfloat16 [256, 256], replicated, may hold values from -0.375 to 0.375
- block_index: int32 [8192, 8], P(('row', 'col')), may hold values from 0 to 31, as said below
- live_counts: int32 [8192], P(('row', 'col')), may hold values from 1 to 8, as said below
- adjacency_tiles: bfloat16 [8192, 8, 128, 128], P(('row', 'col')), may hold values from -0.375 to 0.375
- cotangent: bfloat16 [1048576, 256], P(('row', 'col')), may hold values from -1.75 to 1.75
Outputs:
- activations: bfloat16 [1048576, 256], P(('row', 'col'))
- grad_features: bfloat16 [32768, 256], P(('row', 'col'))
- grad_weight: float32 [256, 256], replicated
The draws below stay inside these ranges and needn't reach their ends.
Inputs may be any that keep to these rules, and one draw needn't show every extreme that they name: Within each row group of 4096 consecutive entries the values are a permutation; the 128 rows of one device name the position block reorder_target // 128 at most 8 times each, and exactly 8 times for some block in every row group. `block_index`: the 8 entries of a row are different source blocks. A destination block uses the first live_counts entries of its row of block_index and of adjacency_tiles; 8 is reached in every draw.
All inputs are finite; a program needn't handle non-finite values.
Results may differ from the reference program's by a relative error of at most 0.02.
Values may be sent and summed in bfloat16 or wider, within the bound.
No kernel may reach another device: no remote copies, remote signals or barrier semaphores. Data moves between devices by JAX's collectives and lax.ppermute only.
A program may use at most 128 MiB of HBM per device.

```python
import jax
import jax.numpy as jnp
from jax import lax

FIN = 256
FOUT = 256
BLK = 128
NBR = 8
SRC_DEV = 128
OWNERS = 32
GROUPS = 8
GROUP_ROWS = 4096
SRC_ROWS = 32768
NSB = 32
DB_DEV = 32
DST_ROWS = 1048576
DST_BLOCKS = 8192


def target_group(group_key):
    key_list = jax.random.split(group_key, 7)
    half_count = OWNERS // 2
    average = SRC_DEV // OWNERS
    spread = jax.random.randint(key_list[0], (half_count,), -average, average + 1)
    chosen = jax.random.randint(key_list[1], (), 0, half_count)
    spread = jnp.where(jnp.arange(half_count) == chosen, average, spread)
    paired = jnp.stack([average + spread, average - spread], axis=1).reshape(OWNERS)
    multiplicity = paired[jax.random.permutation(key_list[2], OWNERS)]
    boundary = jnp.cumsum(multiplicity)
    row_number = jnp.arange(SRC_DEV)
    offsets = jnp.sum((row_number[:, None] >= boundary[None, :]).astype(jnp.int32), axis=1)
    device_keys = jax.random.split(key_list[3], OWNERS)

    def shuffle_rows(device_key):
        return offsets[jax.random.permutation(device_key, SRC_DEV)]
    shuffled = jax.vmap(shuffle_rows)(device_keys)
    rotation = jax.random.permutation(key_list[4], OWNERS)
    relabel = jax.random.permutation(key_list[5], OWNERS)
    owner_index = relabel[(rotation[:, None] + shuffled) % OWNERS].reshape(GROUP_ROWS)
    jitter_keys = jax.random.randint(key_list[6], (GROUP_ROWS,), 0, 2 ** 20)
    sorted_order = jnp.argsort(owner_index * 2 ** 20 + jitter_keys, stable=True)
    return jnp.argsort(sorted_order, stable=True).astype(jnp.int32)


def draw_reorder_target(key, part):
    key = jax.random.fold_in(key, 11)
    return jax.vmap(target_group)(jax.random.split(key, GROUPS)).reshape(SRC_ROWS).astype(jnp.int32)


def draw_block_index(key, part):
    key = jax.random.fold_in(key, 23)
    scores = jax.random.randint(key, (DST_BLOCKS, NSB), 0, 2 ** 16) * NSB + jnp.arange(NSB, dtype=jnp.int32)[None, :]
    return jnp.argsort(scores, axis=1, stable=True)[:, :NBR].astype(jnp.int32)


def draw_live_counts(key, part):
    key = jax.random.fold_in(key, 37)
    key_list = jax.random.split(key, 5)
    devices_all = DST_BLOCKS // DB_DEV
    picked_device = jax.random.randint(key_list[1], (), 0, devices_all)
    heavy = (jax.random.randint(key_list[0], (devices_all,), 0, 4) == 0) | (jnp.arange(devices_all) == picked_device)
    strong = jax.random.randint(key_list[2], (devices_all, DB_DEV), NBR // 2, NBR + 1)
    weak = jax.random.randint(key_list[3], (devices_all, DB_DEV), 1, NBR // 4 + 1)
    peak_slot = jax.random.randint(key_list[4], (devices_all, 1), 0, DB_DEV)
    strong = jnp.where(jnp.arange(DB_DEV)[None, :] == peak_slot, NBR, strong)
    return jnp.where(heavy[:, None], strong, weak).reshape(DST_BLOCKS).astype(jnp.int32)


def steps_of(key, extent, cuts, smallest, largest):
    loudness, own = 1.0, jax.random.fold_in(key, 6)
    for axis_at, parts in cuts:
        steps = jnp.exp(jax.random.uniform(jax.random.fold_in(own, axis_at), (parts,), jnp.float32, smallest / len(cuts), largest / len(cuts)))
        loudness = loudness * jnp.repeat(steps, extent[axis_at] // parts).reshape([-1 if axis == axis_at else 1 for axis in range(len(extent))])
    return loudness


def normal_values(rng, dims, width, reach, cuts=(), held_as=jnp.bfloat16):
    gain = steps_of(rng, dims, cuts, -0.22, 0.18) if cuts else 1.0
    entries = jax.random.normal(rng, dims, jnp.float32) * width * gain
    return jnp.minimum(jnp.maximum(entries, -reach), reach).astype(held_as)


def setup_inputs(seed: int = 0) -> dict:
    arg_keys = jax.random.split(jax.random.key(seed), 8)
    node_features = normal_values(arg_keys[0], (SRC_ROWS, FIN), 1.0, 6.0, ((0, 256),))
    reorder_target = draw_reorder_target(jax.random.fold_in(arg_keys[7], 71), 0)
    weight_matrix = normal_values(arg_keys[2], (FIN, FOUT), FIN ** -0.5, 0.375)
    block_index = draw_block_index(jax.random.fold_in(arg_keys[7], 71), 0)
    live_counts = draw_live_counts(jax.random.fold_in(arg_keys[7], 71), 0)
    adjacency_tiles = normal_values(arg_keys[5], (DST_BLOCKS, NBR, BLK, BLK), (2 * BLK) ** -0.5, 0.375, ((0, 256),))
    cotangent = normal_values(arg_keys[6], (DST_ROWS, FOUT), 0.3, 1.75, ((0, 256),))
    return {"node_features": node_features, "reorder_target": reorder_target, "weight_matrix": weight_matrix, "block_index": block_index, "live_counts": live_counts, "adjacency_tiles": adjacency_tiles, "cotangent": cotangent}


def silu_slope(argument_value):
    logistic = jax.nn.sigmoid(argument_value)
    return logistic * (1.0 + argument_value * (1.0 - logistic))


def place_rows(positions, values):
    return jnp.zeros_like(values).at[positions].set(values)


def take_rows(values, positions):
    return values[positions]


def reference(node_features, reorder_target, weight_matrix, block_index, live_counts, adjacency_tiles, cotangent):
    projected = jnp.dot(node_features, weight_matrix, preferred_element_type=jnp.float32).astype(jnp.bfloat16)
    grouped_target = reorder_target.reshape(GROUPS, GROUP_ROWS)
    grouped_rows = projected.reshape(GROUPS, GROUP_ROWS, FOUT)
    reordered = jax.vmap(place_rows)(grouped_target, grouped_rows).reshape(GROUPS, NSB, BLK, FOUT)
    block_batch = 8
    step_total = DST_BLOCKS // block_batch
    group_of = (jnp.arange(DST_BLOCKS, dtype=jnp.int32) // (OWNERS * DB_DEV)).reshape(step_total, block_batch)
    alive_mask = jnp.arange(NBR, dtype=jnp.int32)[None, :] < live_counts[:, None]
    tiles_view = adjacency_tiles.reshape(step_total, block_batch, NBR, BLK, BLK)
    index_view = block_index.reshape(step_total, block_batch, NBR)
    alive_view = alive_mask.reshape(step_total, block_batch, NBR)

    def forward_step(step_items):
        tile_set, index_set, alive_set, group_set = step_items
        picked = reordered[group_set[:, None], index_set].astype(jnp.float32)
        weights = jnp.where(alive_set[:, :, None, None], tile_set.astype(jnp.float32), 0.0)
        return jnp.einsum('bjuv,bjvf->buf', weights, picked)

    aggregated = lax.map(forward_step, (tiles_view, index_view, alive_view, group_of)).reshape(DST_ROWS, FOUT)
    activations = jax.nn.silu(aggregated).astype(jnp.bfloat16)
    pre_grad = (cotangent.astype(jnp.float32) * silu_slope(aggregated)).astype(jnp.bfloat16)
    run_total = DST_BLOCKS // DB_DEV
    run_tiles = adjacency_tiles.reshape(run_total, DB_DEV, NBR, BLK, BLK)
    run_index = block_index.reshape(run_total, DB_DEV, NBR)
    run_alive = alive_mask.reshape(run_total, DB_DEV, NBR)
    run_grad = pre_grad.reshape(run_total, DB_DEV, BLK, FOUT)
    run_group = jnp.arange(run_total, dtype=jnp.int32) // OWNERS

    def backward_step(running, step_items):
        tile_set, index_set, alive_set, grad_set, group_one = step_items
        weights = jnp.where(alive_set[:, :, None, None], tile_set.astype(jnp.float32), 0.0)
        contrib = jnp.einsum('bjuv,buf->bjvf', weights, grad_set.astype(jnp.float32))
        partial_value = jnp.zeros((NSB, BLK, FOUT), jnp.float32).at[index_set.reshape(-1)].add(contrib.reshape(-1, BLK, FOUT))
        rounded = lax.optimization_barrier(partial_value.astype(jnp.bfloat16)).astype(jnp.float32)
        running = running.at[group_one].add(rounded)
        return running, None

    start_total = jnp.zeros((GROUPS, NSB, BLK, FOUT), jnp.float32)
    reordered_grad, unused = lax.scan(backward_step, start_total, (run_tiles, run_index, run_alive, run_grad, run_group))
    reordered_grad = reordered_grad.reshape(GROUPS, GROUP_ROWS, FOUT)
    projected_grad = jax.vmap(take_rows)(reordered_grad, grouped_target).reshape(SRC_ROWS, FOUT).astype(jnp.bfloat16)
    grad_features = jnp.dot(projected_grad, weight_matrix.T, preferred_element_type=jnp.float32).astype(jnp.bfloat16)
    grad_weight = jnp.dot(node_features.T, projected_grad, preferred_element_type=jnp.float32) * (SRC_ROWS ** -0.5)
    return (activations, grad_features, grad_weight)
```

```python
import functools

import jax
import jax.numpy as jnp
from jax import lax
from jax.experimental import pallas as pl
from jax.experimental.pallas import tpu as pltpu
from jax.sharding import PartitionSpec as P

BF = jnp.bfloat16
F32 = jnp.float32
META = 16
STEP_BLOCKS = 4


def dot(a, b, ca=1, cb=0):
    return lax.dot_general(a, b, (((ca,), (cb,)), ((), ())), preferred_element_type=F32)


def layer_kernel(
    idx_ref,
    core_ref,
    own_ref,
    oth_ref,
    w_ref,
    adj_ref,
    cot_ref,
    act_ref,
    rs_own_ref,
    rs_oth_ref,
    slots,
    src,
    feats,
    part,
    gw,
):
    chips, rows, width = own_ref.shape[0], own_ref.shape[1] - META, own_ref.shape[2]
    owners = 2 * chips
    cap = slots.shape[1] // owners
    nbr = adj_ref.shape[1]
    step = pl.program_id(0)

    def one_hots(ref, i):
        meta = ref[i, rows : rows + META, :].astype(F32)
        slot_row = meta[0:1, :rows]
        place_row = meta[0:1, rows : 2 * rows]
        slot_id = lax.broadcasted_iota(jnp.int32, (owners * cap, rows), 0).astype(F32)
        place_id = lax.broadcasted_iota(jnp.int32, (rows, rows), 0).astype(F32)
        to_slot = jnp.where(slot_id == slot_row, 1.0, 0.0).astype(BF)
        to_place = jnp.where(place_id == place_row, 1.0, 0.0).astype(BF)
        return to_slot, to_place

    @pl.when(step == 0)
    def _():
        part[...] = jnp.zeros_like(part)
        src[owners] = jnp.zeros(src.shape[1:], BF)

        for side, ref in enumerate((own_ref, oth_ref)):

            def spread_rows(i, carry):
                to_slot, to_place = one_hots(ref, i)
                s = side * chips + i
                at = pl.ds(pl.multiple_of(s * cap, cap), cap)
                moved = dot(to_slot, ref[i, :rows, :])
                slots[:, at, :width] = moved.reshape(owners, cap, width)
                table = dot(to_slot, to_place, 1, 1)
                slots[:, at, width:] = table.reshape(owners, cap, rows)
                return carry

            lax.fori_loop(0, chips, spread_rows, 0, unroll=2)

        def place_rows(p, carry):
            table = slots[p, :, width:].astype(BF)
            block = dot(table, slots[p, :, :width].astype(BF), 0, 0).astype(BF)
            feats[p] = block
            src[p] = dot(block, w_ref[...]).astype(BF)
            return carry

        lax.fori_loop(0, owners, place_rows, 0, unroll=2)

    for k in range(STEP_BLOCKS):
        base = (step * STEP_BLOCKS + k) * nbr
        ids = [idx_ref[base + j] for j in range(nbr)]
        tiles = [
            jnp.concatenate([adj_ref[k, 2 * q], adj_ref[k, 2 * q + 1]], axis=1)
            for q in range(nbr // 2)
        ]
        v = None
        for q in range(nbr // 2):
            picked = jnp.concatenate([src[ids[2 * q]], src[ids[2 * q + 1]]], axis=0)
            term = dot(tiles[q], picked)
            v = term if v is None else v + term
        here = pl.ds(k * rows, rows)
        s = 1.0 / (1.0 + jnp.exp(-v))
        act_ref[here, :] = (v * s).astype(BF)
        slope = s * (1.0 + v * (1.0 - s))
        grad = (cot_ref[here, :].astype(F32) * slope).T.astype(BF)
        for q in range(nbr // 2):
            contrib = dot(grad, tiles[q])
            a, b = ids[2 * q], ids[2 * q + 1]
            old_a, old_b = part[a], part[b]
            part[a] = old_a + contrib[:, :rows]
            part[b] = old_b + contrib[:, rows:]

    @pl.when(step == pl.num_programs(0) - 1)
    def _():
        gw[...] = jnp.zeros_like(gw)

        def to_slots(p, carry):
            grad = part[p].astype(BF)
            gw[...] += dot(grad, feats[p])
            table = slots[p, :, width:].astype(BF)
            slots[p, :, :width] = dot(table, grad, 1, 1)
            return carry

        lax.fori_loop(0, owners, to_slots, 0, unroll=2)
        gw[...] = gw[...].T
        core = core_ref[0]
        share = width // owners
        for side, (ref, out) in enumerate(((own_ref, rs_own_ref), (oth_ref, rs_oth_ref))):

            def collect_rows(i, carry):
                to_slot, _ = one_hots(ref, i)
                s = side * chips + i
                at = pl.ds(pl.multiple_of(s * cap, cap), cap)
                held = slots[:, at, :width].reshape(owners * cap, width).astype(BF)
                out[i, :rows, :] = dot(to_slot, held, 0, 0).astype(BF)
                device = 2 * i + (core if side == 0 else 1 - core)
                g = gw[pl.ds(pl.multiple_of(device * share, share), share), :]
                high = g.astype(BF).astype(F32)
                out[i, rows:, :] = jnp.concatenate([high, g - high], axis=0).astype(BF)
                return carry

            lax.fori_loop(0, chips, collect_rows, 0, unroll=2)


def layer(ids, core, own, oth, w, adj, cot):
    chips, padded, width = own.shape
    rows = padded - META
    owners = 2 * chips
    blocks, nbr = adj.shape[:2]
    cap = 2 * rows // owners
    steps = blocks // STEP_BLOCKS
    whole = lambda shape: pl.BlockSpec(shape, lambda t, *_: (0,) * len(shape))
    grid_spec = pltpu.PrefetchScalarGridSpec(
        num_scalar_prefetch=2,
        grid=(steps,),
        in_specs=[
            whole(own.shape),
            whole(oth.shape),
            whole(w.shape),
            pl.BlockSpec((STEP_BLOCKS, nbr, rows, rows), lambda t, *_: (t, 0, 0, 0)),
            pl.BlockSpec((STEP_BLOCKS * rows, width), lambda t, *_: (t, 0)),
        ],
        out_specs=[
            pl.BlockSpec((STEP_BLOCKS * rows, width), lambda t, *_: (t, 0)),
            whole(own.shape),
            whole(own.shape),
        ],
        scratch_shapes=[
            pltpu.VMEM((owners, owners * cap, width + rows), F32),
            pltpu.VMEM((owners + 1, rows, width), BF),
            pltpu.VMEM((owners, rows, width), BF),
            pltpu.VMEM((owners + 1, width, rows), F32),
            pltpu.VMEM((width, width), F32),
        ],
    )
    return pl.pallas_call(
        layer_kernel,
        grid_spec=grid_spec,
        out_shape=[
            jax.ShapeDtypeStruct(cot.shape, BF),
            jax.ShapeDtypeStruct(own.shape, BF),
            jax.ShapeDtypeStruct(own.shape, BF),
        ],
        compiler_params=pltpu.CompilerParams(
            dimension_semantics=("arbitrary",), vmem_limit_bytes=56 * 1024 * 1024
        ),
    )(ids, core, own, oth, w, adj, cot)


def on_device(
    node_features,
    reorder_target,
    weight_matrix,
    block_index,
    live_counts,
    adjacency_tiles,
    cotangent,
):
    cols = lax.axis_size("col")
    zs = lax.axis_size("row")
    chips = cols // 2
    rows, width = node_features.shape
    total_rows = rows * cols * zs
    nbr = adjacency_tiles.shape[1]
    swap = [(i, i ^ 1) for i in range(cols)]
    same_core = [[2 * i + c for i in range(chips)] for c in range(2)]
    core = lax.axis_index("col") % 2

    owner = reorder_target // rows
    place = reorder_target % rows
    earlier = jnp.arange(rows)[:, None] < jnp.arange(rows)[None, :]
    rank = jnp.sum((owner[:, None] == owner[None, :]) & earlier, axis=0, dtype=jnp.int32)
    cap = 2 * rows // cols
    meta = jnp.concatenate([owner * cap + rank, place]).astype(BF)[None, :]
    block = jnp.concatenate([node_features, jnp.broadcast_to(meta, (META, width))], axis=0)
    own = lax.all_to_all(
        jnp.broadcast_to(block[None], (chips,) + block.shape),
        "col",
        0,
        0,
        tiled=True,
        axis_index_groups=same_core,
    )
    oth = lax.ppermute(own, "col", swap)
    alive = jnp.arange(nbr, dtype=jnp.int32)[None, :] < live_counts[:, None]
    ids = jnp.where(alive, block_index, cols).reshape(-1)

    activations, rs_own, rs_oth = layer(
        ids, core.reshape(1), own, oth, weight_matrix, adjacency_tiles, cotangent
    )
    got = lax.ppermute(rs_oth, "col", swap)
    both = rs_own.astype(F32) + got.astype(F32)
    share = META // 2
    weight_part = both[:, rows : rows + share] + both[:, rows + share :]
    high = weight_part.astype(BF)
    low = (weight_part - high.astype(F32)).astype(BF)
    pair = jnp.concatenate([both[:, :rows].astype(BF), high, low], axis=1)
    landed = lax.all_to_all(pair, "col", 0, 0, tiled=True, axis_index_groups=same_core)
    summed = jnp.sum(landed.astype(F32), axis=0)
    projected_grad = summed[:rows].astype(BF)
    grad_features = dot(projected_grad, weight_matrix, 1, 1).astype(BF)
    weight_rows = summed[rows : rows + share] + summed[rows + share :]
    by_row = lax.all_to_all(
        jnp.broadcast_to(weight_rows[None], (zs,) + weight_rows.shape), "row", 0, 0, tiled=True
    )
    weight_rows = jnp.sum(by_row, axis=0) * total_rows ** (-0.5)
    by_col = lax.all_to_all(
        jnp.broadcast_to(weight_rows[None], (cols,) + weight_rows.shape), "col", 0, 0, tiled=True
    )
    return activations, grad_features, by_col.reshape(width, width)


def solution(mesh):
    return jax.shard_map(
        on_device,
        mesh=mesh,
        in_specs=(
            P(("row", "col"), None),
            P(("row", "col")),
            P(),
            P(("row", "col"), None),
            P(("row", "col")),
            P(("row", "col"), None, None, None),
            P(("row", "col"), None),
        ),
        out_specs=(P(("row", "col"), None), P(("row", "col"), None), P()),
        check_vma=False,
    )
```

```python
import functools

import jax
import jax.numpy as jnp
from jax import lax
from jax.experimental import pallas as pl
from jax.experimental.pallas import tpu as pltpu
from jax.sharding import PartitionSpec as P

BF = jnp.bfloat16
F32 = jnp.float32
META = 16
GROUP = 16
SIDE = 4
UNROLL = 16


def dot(a, b, ca=1, cb=0):
    return lax.dot_general(a, b, (((ca,), (cb,)), ((), ())), preferred_element_type=F32)


def layer_kernel(
    idx_ref,
    me_ref,
    own_ref,
    oth_ref,
    w_ref,
    adj_hbm,
    cot_hbm,
    act_hbm,
    rs_own_ref,
    rs_oth_ref,
    gw,
    adj_ref,
    cot_ref,
    act_ref,
    slots,
    src,
    feats,
    part,
    adj_sem,
    cot_sem,
    act_sem,
):
    chips, rows, width = own_ref.shape[0], own_ref.shape[1] - META, own_ref.shape[2]
    owners = 2 * chips
    cap = slots.shape[1] // owners
    blocks, nbr = adj_ref.shape[:2]
    groups = blocks // GROUP

    def fetch(g):
        at = pl.ds(g * GROUP, GROUP)
        band = pl.ds(g * GROUP * rows, GROUP * rows)
        return (
            pltpu.make_async_copy(adj_hbm.at[at], adj_ref.at[at], adj_sem.at[g]),
            pltpu.make_async_copy(cot_hbm.at[band], cot_ref.at[band], cot_sem.at[g]),
        )

    def flush(g):
        band = pl.ds(g * GROUP * rows, GROUP * rows)
        return pltpu.make_async_copy(act_ref.at[band], act_hbm.at[band], act_sem.at[g])

    for g in range(groups):
        for copy in fetch(g):
            copy.start()

    def one_hots(ref, i):
        meta = ref[i, rows : rows + META, :].astype(F32)
        slot_row = meta[0:1, :rows]
        place_row = meta[0:1, rows : 2 * rows]
        slot_id = lax.broadcasted_iota(jnp.int32, (owners * cap, rows), 0).astype(F32)
        place_id = lax.broadcasted_iota(jnp.int32, (rows, rows), 0).astype(F32)
        to_slot = jnp.where(slot_id == slot_row, 1.0, 0.0).astype(BF)
        to_place = jnp.where(place_id == place_row, 1.0, 0.0).astype(BF)
        return to_slot, to_place

    part[...] = jnp.zeros_like(part)
    src[owners] = jnp.zeros(src.shape[1:], BF)

    for side, ref in enumerate((own_ref, oth_ref)):

        def spread_rows(i, carry):
            to_slot, to_place = one_hots(ref, i)
            s = side * chips + i
            at = pl.ds(pl.multiple_of(s * cap, cap), cap)
            moved = dot(to_slot, ref[i, :rows, :])
            slots[:, at, :width] = moved.reshape(owners, cap, width)
            table = dot(to_slot, to_place, 1, 1)
            slots[:, at, width:] = table.reshape(owners, cap, rows)
            return carry

        lax.fori_loop(0, chips, spread_rows, 0, unroll=UNROLL)

    def place_rows(p, carry):
        table = slots[p, :, width:].astype(BF)
        block = dot(table, slots[p, :, :width].astype(BF), 0, 0).astype(BF)
        feats[p] = block
        src[p] = dot(block, w_ref[...]).astype(BF)
        return carry

    lax.fori_loop(0, owners, place_rows, 0, unroll=UNROLL)

    def forward(b):
        ids = [idx_ref[b * nbr + j] for j in range(nbr)]
        tiles = [
            jnp.concatenate([adj_ref[b, 2 * q], adj_ref[b, 2 * q + 1]], axis=1)
            for q in range(nbr // 2)
        ]
        v = None
        for q in range(nbr // 2):
            picked = jnp.concatenate([src[ids[2 * q]], src[ids[2 * q + 1]]], axis=0)
            term = dot(tiles[q], picked)
            v = term if v is None else v + term
        return ids, tiles, v

    def middle(b, v):
        here = pl.ds(pl.multiple_of(b * rows, rows), rows)
        s = 1.0 / (1.0 + jnp.exp(-v))
        act_ref[here, :] = (v * s).astype(BF)
        slope = s * (1.0 + v * (1.0 - s))
        return (cot_ref[here, :].astype(F32) * slope).T.astype(BF)

    def backward(ids, tiles, grad):
        for q in range(nbr // 2):
            contrib = dot(grad, tiles[q])
            a, b = ids[2 * q], ids[2 * q + 1]
            old_a, old_b = part[a], part[b]
            part[a] = old_a + contrib[:, :rows]
            part[b] = old_b + contrib[:, rows:]

    def run_group(g, carry):
        for copy in fetch(g):
            copy.wait()
        ahead = forward(g * GROUP)
        for k in range(GROUP):
            grad = middle(g * GROUP + k, ahead[2])
            later = forward(g * GROUP + k + 1) if k + 1 < GROUP else None
            backward(ahead[0], ahead[1], grad)
            ahead = later
        flush(g).start()
        return carry

    lax.fori_loop(0, groups, run_group, 0)

    gw[...] = jnp.zeros_like(gw)

    def to_slots(p, carry):
        grad = part[p].astype(BF)
        gw[...] += dot(grad, feats[p])
        table = slots[p, :, width:].astype(BF)
        slots[p, :, :width] = dot(table, grad, 1, 1)
        return carry

    lax.fori_loop(0, owners, to_slots, 0, unroll=UNROLL)
    gw[...] = gw[...].T
    my_y, my_x = me_ref[0], me_ref[1]
    for side, (ref, out) in enumerate(((own_ref, rs_own_ref), (oth_ref, rs_oth_ref))):

        def collect_rows(i, carry):
            to_slot, _ = one_hots(ref, i)
            s = side * chips + i
            at = pl.ds(pl.multiple_of(s * cap, cap), cap)
            held = slots[:, at, :width].reshape(owners * cap, width).astype(BF)
            away_y = (i // SIDE + SIDE - my_y) % SIDE
            away_x = (i % SIDE + SIDE - my_x) % SIDE
            out[away_x * SIDE + away_y] = dot(to_slot, held, 0, 0).astype(BF)
            return carry

        lax.fori_loop(0, chips, collect_rows, 0, unroll=UNROLL)

    for g in range(groups):
        flush(g).wait()


def layer(ids, me, own, oth, w, adj, cot):
    chips, padded, width = own.shape
    rows = padded - META
    owners = 2 * chips
    blocks, nbr = adj.shape[:2]
    cap = 2 * rows // owners
    groups = blocks // GROUP
    vmem = pl.BlockSpec(memory_space=pltpu.VMEM)
    smem = pl.BlockSpec(memory_space=pltpu.SMEM)
    hbm = pl.BlockSpec(memory_space=pl.ANY)
    return pl.pallas_call(
        layer_kernel,
        in_specs=[smem, smem, vmem, vmem, vmem, hbm, hbm],
        out_specs=[hbm, vmem, vmem, vmem],
        out_shape=[
            jax.ShapeDtypeStruct(cot.shape, BF),
            jax.ShapeDtypeStruct((chips, rows, width), BF),
            jax.ShapeDtypeStruct((chips, rows, width), BF),
            jax.ShapeDtypeStruct((width, width), F32),
        ],
        scratch_shapes=[
            pltpu.VMEM(adj.shape, BF),
            pltpu.VMEM(cot.shape, BF),
            pltpu.VMEM(cot.shape, BF),
            pltpu.VMEM((owners, owners * cap, width + rows), F32),
            pltpu.VMEM((owners + 1, rows, width), BF),
            pltpu.VMEM((owners, rows, width), BF),
            pltpu.VMEM((owners + 1, width, rows), F32),
            pltpu.SemaphoreType.DMA((groups,)),
            pltpu.SemaphoreType.DMA((groups,)),
            pltpu.SemaphoreType.DMA((groups,)),
        ],
        compiler_params=pltpu.CompilerParams(vmem_limit_bytes=56 * 1024 * 1024),
    )(ids, me, own, oth, w, adj, cot)


def on_device(
    node_features,
    reorder_target,
    weight_matrix,
    block_index,
    live_counts,
    adjacency_tiles,
    cotangent,
):
    cols = lax.axis_size("col")
    zs = lax.axis_size("row")
    chips = cols // 2
    rows, width = node_features.shape
    total_rows = rows * cols * zs
    nbr = adjacency_tiles.shape[1]
    swap = [(i, i ^ 1) for i in range(cols)]
    same_core = [[2 * i + c for i in range(chips)] for c in range(2)]
    chip = lax.axis_index("col") // 2

    def shift(dy, dx):
        pairs = []
        for i in range(cols):
            y, x, c = i // (2 * SIDE), i // 2 % SIDE, i % 2
            pairs.append((i, ((y + dy) % SIDE * SIDE + (x + dx) % SIDE) * 2 + c))
        return pairs


    owner = reorder_target // rows
    place = reorder_target % rows
    earlier = jnp.arange(rows)[:, None] < jnp.arange(rows)[None, :]
    rank = jnp.sum((owner[:, None] == owner[None, :]) & earlier, axis=0, dtype=jnp.int32)
    cap = 2 * rows // cols
    meta = jnp.concatenate([owner * cap + rank, place]).astype(BF)[None, :]
    block = jnp.concatenate([node_features, jnp.broadcast_to(meta, (META, width))], axis=0)
    own = lax.all_to_all(
        jnp.broadcast_to(block[None], (chips,) + block.shape),
        "col",
        0,
        0,
        tiled=True,
        axis_index_groups=same_core,
    )
    oth = lax.ppermute(own, "col", swap)
    alive = jnp.arange(nbr, dtype=jnp.int32)[None, :] < live_counts[:, None]
    ids = jnp.where(alive, block_index, cols).reshape(-1)

    place_here = jnp.stack([chip // SIDE, chip % SIDE])
    activations, rs_own, rs_oth, weight_term = layer(
        ids, place_here, own, oth, weight_matrix, adjacency_tiles, cotangent
    )
    got = lax.ppermute(rs_oth, "col", swap)
    both = [
        (rs_own[d * SIDE : (d + 1) * SIDE].astype(F32) + got[d * SIDE : (d + 1) * SIDE].astype(F32))
        for d in range(SIDE)
    ]
    along_x = both[0]
    for d in range(1, SIDE):
        along_x += lax.ppermute(both[d].astype(BF), "col", shift(0, d)).astype(F32)
    summed = along_x[0]
    for d in range(1, SIDE):
        summed += lax.ppermute(along_x[d].astype(BF), "col", shift(d, 0)).astype(F32)
    projected_grad = summed.astype(BF)
    grad_features = dot(projected_grad, weight_matrix, 1, 1).astype(BF)

    share = width // cols
    parts = lax.all_to_all(weight_term.reshape(cols, share, width), "col", 0, 0, tiled=True)
    weight_rows = jnp.sum(parts, axis=0)
    by_row = lax.all_to_all(
        jnp.broadcast_to(weight_rows[None], (zs,) + weight_rows.shape), "row", 0, 0, tiled=True
    )
    weight_rows = jnp.sum(by_row, axis=0) * total_rows ** (-0.5)
    by_col = lax.all_to_all(
        jnp.broadcast_to(weight_rows[None], (cols,) + weight_rows.shape), "col", 0, 0, tiled=True
    )
    return activations, grad_features, by_col.reshape(width, width)


def solution(mesh):
    return jax.shard_map(
        on_device,
        mesh=mesh,
        in_specs=(
            P(("row", "col"), None),
            P(("row", "col")),
            P(),
            P(("row", "col"), None),
            P(("row", "col")),
            P(("row", "col"), None, None, None),
            P(("row", "col"), None),
        ),
        out_specs=(P(("row", "col"), None), P(("row", "col"), None), P()),
        check_vma=False,
    )
```

```python
import functools

import jax
import jax.numpy as jnp
from jax import lax
from jax.experimental import pallas as pl
from jax.experimental.pallas import tpu as pltpu
from jax.sharding import PartitionSpec as P

BF = jnp.bfloat16
F32 = jnp.float32
META = 16
GROUP = 16
SIDE = 4
UNROLL = 16


def dot(a, b, ca=1, cb=0):
    return lax.dot_general(a, b, (((ca,), (cb,)), ((), ())), preferred_element_type=F32)


def one_hot(ids, count):
    rows = lax.broadcasted_iota(jnp.int32, (count, ids.shape[1]), 0).astype(F32)
    return jnp.where(rows == ids, 1.0, 0.0).astype(BF)


def layer_kernel(
    idx_ref,
    own_hbm,
    oth_hbm,
    w_ref,
    adj_hbm,
    cot_hbm,
    act_hbm,
    table_hbm,
    part_hbm,
    meta_own_hbm,
    meta_oth_hbm,
    gw,
    own_ref,
    oth_ref,
    table_ref,
    sent_ref,
    adj_ref,
    cot_ref,
    act_ref,
    slots,
    src,
    feats,
    part,
    row_sem,
    adj_sem,
    cot_sem,
    act_sem,
):
    chips, rows, width = own_ref.shape[0], own_ref.shape[1] - META, own_ref.shape[2]
    owners = 2 * chips
    cap = slots.shape[1] // owners
    blocks, nbr = adj_ref.shape[:2]
    groups = blocks // GROUP

    def fetch(g):
        at = pl.ds(g * GROUP, GROUP)
        band = pl.ds(g * GROUP * rows, GROUP * rows)
        return (
            pltpu.make_async_copy(adj_hbm.at[at], adj_ref.at[at], adj_sem.at[g]),
            pltpu.make_async_copy(cot_hbm.at[band], cot_ref.at[band], cot_sem.at[g]),
        )

    def flush(g):
        band = pl.ds(g * GROUP * rows, GROUP * rows)
        return pltpu.make_async_copy(act_ref.at[band], act_hbm.at[band], act_sem.at[g])

    take_own = pltpu.make_async_copy(own_hbm, own_ref, row_sem.at[0])
    take_oth = pltpu.make_async_copy(oth_hbm, oth_ref, row_sem.at[1])
    tail = pl.ds(rows, META)
    give_metas = (
        pltpu.make_async_copy(own_ref.at[:, tail], meta_own_hbm, row_sem.at[5]),
        pltpu.make_async_copy(oth_ref.at[:, tail], meta_oth_hbm, row_sem.at[6]),
    )
    give_table = pltpu.make_async_copy(table_ref, table_hbm, row_sem.at[2])

    def give_part(h):
        at = pl.ds(h * chips, chips)
        return pltpu.make_async_copy(sent_ref.at[at], part_hbm.at[at], row_sem.at[3 + h])

    take_own.start()
    take_oth.start()
    for g in range(groups):
        for copy in fetch(g):
            copy.start()

    part[...] = jnp.zeros_like(part)
    src[owners] = jnp.zeros(src.shape[1:], BF)

    for side, (ref, take) in enumerate(((own_ref, take_own), (oth_ref, take_oth))):
        take.wait()

        def spread_rows(i, carry):
            meta = ref[i, rows : rows + META, :].astype(F32)
            to_slot = one_hot(meta[0:1, :rows], owners * cap)
            to_place = one_hot(meta[0:1, rows : 2 * rows], rows)
            s = side * chips + i
            at = pl.ds(pl.multiple_of(s * cap, cap), cap)
            moved = dot(to_slot, ref[i, :rows, :])
            slots[:, at, :width] = moved.reshape(owners, cap, width)
            table = dot(to_slot, to_place, 1, 1)
            slots[:, at, width:] = table.reshape(owners, cap, rows)
            return carry

        lax.fori_loop(0, chips, spread_rows, 0, unroll=UNROLL)

    def place_rows(p, carry):
        table = slots[p, :, width:].astype(BF)
        table_ref[p] = table
        block = dot(table, slots[p, :, :width].astype(BF), 0, 0).astype(BF)
        feats[p] = block
        src[p] = dot(block, w_ref[...]).astype(BF)
        return carry

    lax.fori_loop(0, owners, place_rows, 0, unroll=UNROLL)
    give_table.start()
    for give in give_metas:
        give.start()

    def forward(b):
        ids = [idx_ref[b * nbr + j] for j in range(nbr)]
        tiles = [
            jnp.concatenate([adj_ref[b, 2 * q], adj_ref[b, 2 * q + 1]], axis=1)
            for q in range(nbr // 2)
        ]
        v = None
        for q in range(nbr // 2):
            picked = jnp.concatenate([src[ids[2 * q]], src[ids[2 * q + 1]]], axis=0)
            term = dot(tiles[q], picked)
            v = term if v is None else v + term
        return ids, tiles, v

    def middle(b, v):
        here = pl.ds(pl.multiple_of(b * rows, rows), rows)
        s = 1.0 / (1.0 + jnp.exp(-v))
        act_ref[here, :] = (v * s).astype(BF)
        slope = s * (1.0 + v * (1.0 - s))
        return (cot_ref[here, :].astype(F32) * slope).astype(BF)

    def backward(ids, tiles, grad):
        for q in range(nbr // 2):
            contrib = dot(tiles[q], grad, 0, 0)
            a, b = ids[2 * q], ids[2 * q + 1]
            old_a, old_b = part[a], part[b]
            part[a] = old_a + contrib[:rows]
            part[b] = old_b + contrib[rows:]

    def run_group(g, carry):
        for copy in fetch(g):
            copy.wait()
        ahead = forward(g * GROUP)
        for k in range(GROUP):
            grad = middle(g * GROUP + k, ahead[2])
            later = forward(g * GROUP + k + 1) if k + 1 < GROUP else None
            backward(ahead[0], ahead[1], grad)
            ahead = later
        flush(g).start()
        return carry

    lax.fori_loop(0, groups, run_group, 0)

    gw[...] = jnp.zeros_like(gw)

    def weight_term(p, carry):
        grad = part[p].astype(BF)
        sent_ref[p] = grad
        gw[...] += dot(feats[p], grad, 0, 0)
        return carry

    for h in range(2):
        lax.fori_loop(h * chips, (h + 1) * chips, weight_term, 0, unroll=UNROLL)
        give_part(h).start()

    for g in range(groups):
        flush(g).wait()
    give_table.wait()
    for give in give_metas:
        give.wait()
    for h in range(2):
        give_part(h).wait()


def return_kernel(
    me_ref,
    meta_own_hbm,
    meta_oth_hbm,
    table_hbm,
    part_hbm,
    rs_own_hbm,
    rs_oth_hbm,
    meta_own,
    meta_oth,
    table_ref,
    part_ref,
    rs_own_ref,
    rs_oth_ref,
    slots,
    meta_sem,
    part_sem,
    give_sem,
):
    chips, rows, width = rs_own_ref.shape
    owners = 2 * chips
    cap = slots.shape[1] // owners

    def take(h):
        at = pl.ds(h * chips, chips)
        return (
            pltpu.make_async_copy(table_hbm.at[at], table_ref.at[at], part_sem.at[2 * h]),
            pltpu.make_async_copy(part_hbm.at[at], part_ref.at[at], part_sem.at[2 * h + 1]),
        )

    metas = (
        pltpu.make_async_copy(meta_own_hbm, meta_own, meta_sem.at[0]),
        pltpu.make_async_copy(meta_oth_hbm, meta_oth, meta_sem.at[1]),
    )
    for copy in (*take(0), *take(1), *metas):
        copy.start()

    def to_slots(p, carry):
        slots[p] = dot(table_ref[p], part_ref[p])
        return carry

    for h in range(2):
        for copy in take(h):
            copy.wait()
        lax.fori_loop(h * chips, (h + 1) * chips, to_slots, 0, unroll=UNROLL)

    for copy in metas:
        copy.wait()
    my_y, my_x = me_ref[0], me_ref[1]
    gives = []
    for side, meta_ref, out, hbm in (
        (1, meta_oth, rs_oth_ref, rs_oth_hbm),
        (0, meta_own, rs_own_ref, rs_own_hbm),
    ):

        def collect_rows(i, carry):
            to_slot = one_hot(meta_ref[i].astype(F32)[0:1, :rows], owners * cap)
            s = side * chips + i
            at = pl.ds(pl.multiple_of(s * cap, cap), cap)
            held = slots[:, at, :].reshape(owners * cap, width).astype(BF)
            away_y = (i // SIDE + SIDE - my_y) % SIDE
            away_x = (i % SIDE + SIDE - my_x) % SIDE
            out[away_x * SIDE + away_y] = dot(to_slot, held, 0, 0).astype(BF)
            return carry

        lax.fori_loop(0, chips, collect_rows, 0, unroll=UNROLL)
        give = pltpu.make_async_copy(out, hbm, give_sem.at[side])
        give.start()
        gives.append(give)
    for give in gives:
        give.wait()


def return_rows(me, meta_own, meta_oth, table, part):
    chips, rows, width = part.shape[0] // 2, *part.shape[1:]
    owners = 2 * chips
    smem = pl.BlockSpec(memory_space=pltpu.SMEM)
    hbm = pl.BlockSpec(memory_space=pl.ANY)
    back = jax.ShapeDtypeStruct((chips, rows, width), BF)
    return pl.pallas_call(
        return_kernel,
        in_specs=[smem, hbm, hbm, hbm, hbm],
        out_specs=[hbm, hbm],
        out_shape=[back, back],
        scratch_shapes=[
            pltpu.VMEM((chips, META, width), BF),
            pltpu.VMEM((chips, META, width), BF),
            pltpu.VMEM(table.shape, BF),
            pltpu.VMEM(part.shape, BF),
            pltpu.VMEM(back.shape, BF),
            pltpu.VMEM(back.shape, BF),
            pltpu.VMEM((owners, table.shape[1], width), F32),
            pltpu.SemaphoreType.DMA((2,)),
            pltpu.SemaphoreType.DMA((4,)),
            pltpu.SemaphoreType.DMA((2,)),
        ],
        cost_estimate=pl.CostEstimate(
            flops=4 * owners * table.shape[1] * rows * width,
            bytes_accessed=12 * part.size,
            transcendentals=0,
        ),
        compiler_params=pltpu.CompilerParams(vmem_limit_bytes=58 * 1024 * 1024),
    )(me, meta_own, meta_oth, table, part)


def layer(ids, own, oth, w, adj, cot):
    chips, padded, width = own.shape
    rows = padded - META
    owners = 2 * chips
    blocks, nbr = adj.shape[:2]
    cap = 2 * rows // owners
    groups = blocks // GROUP
    vmem = pl.BlockSpec(memory_space=pltpu.VMEM)
    smem = pl.BlockSpec(memory_space=pltpu.SMEM)
    hbm = pl.BlockSpec(memory_space=pl.ANY)
    return pl.pallas_call(
        layer_kernel,
        in_specs=[smem, hbm, hbm, vmem, hbm, hbm],
        out_specs=[hbm, hbm, hbm, hbm, hbm, vmem],
        out_shape=[
            jax.ShapeDtypeStruct(cot.shape, BF),
            jax.ShapeDtypeStruct((owners, owners * cap, rows), BF),
            jax.ShapeDtypeStruct((owners, rows, width), BF),
            jax.ShapeDtypeStruct((chips, META, width), BF),
            jax.ShapeDtypeStruct((chips, META, width), BF),
            jax.ShapeDtypeStruct((width, width), F32),
        ],
        scratch_shapes=[
            pltpu.VMEM(own.shape, BF),
            pltpu.VMEM(own.shape, BF),
            pltpu.VMEM((owners, owners * cap, rows), BF),
            pltpu.VMEM((owners, rows, width), BF),
            pltpu.VMEM(adj.shape, BF),
            pltpu.VMEM(cot.shape, BF),
            pltpu.VMEM(cot.shape, BF),
            pltpu.VMEM((owners, owners * cap, width + rows), F32),
            pltpu.VMEM((owners + 1, rows, width), BF),
            pltpu.VMEM((owners, rows, width), BF),
            pltpu.VMEM((owners + 1, rows, width), F32),
            pltpu.SemaphoreType.DMA((7,)),
            pltpu.SemaphoreType.DMA((groups,)),
            pltpu.SemaphoreType.DMA((groups,)),
            pltpu.SemaphoreType.DMA((groups,)),
        ],
        compiler_params=pltpu.CompilerParams(vmem_limit_bytes=58 * 1024 * 1024),
    )(ids, own, oth, w, adj, cot)


def on_device(
    node_features,
    reorder_target,
    weight_matrix,
    block_index,
    live_counts,
    adjacency_tiles,
    cotangent,
):
    cols = lax.axis_size("col")
    zs = lax.axis_size("row")
    chips = cols // 2
    rows, width = node_features.shape
    total_rows = rows * cols * zs
    nbr = adjacency_tiles.shape[1]
    swap = [(i, i ^ 1) for i in range(cols)]
    same_core = [[2 * i + c for i in range(chips)] for c in range(2)]
    chip = lax.axis_index("col") // 2

    def shift(dy, dx):
        pairs = []
        for i in range(cols):
            y, x, c = i // (2 * SIDE), i // 2 % SIDE, i % 2
            pairs.append((i, ((y + dy) % SIDE * SIDE + (x + dx) % SIDE) * 2 + c))
        return pairs


    owner = reorder_target // rows
    place = reorder_target % rows
    earlier = jnp.arange(rows)[:, None] < jnp.arange(rows)[None, :]
    rank = jnp.sum((owner[:, None] == owner[None, :]) & earlier, axis=0, dtype=jnp.int32)
    cap = 2 * rows // cols
    meta = jnp.concatenate([owner * cap + rank, place]).astype(BF)[None, :]
    block = jnp.concatenate([node_features, jnp.broadcast_to(meta, (META, width))], axis=0)
    own = lax.all_to_all(
        jnp.broadcast_to(block[None], (chips,) + block.shape),
        "col",
        0,
        0,
        tiled=True,
        axis_index_groups=same_core,
    )
    oth = lax.ppermute(own, "col", swap)
    alive = jnp.arange(nbr, dtype=jnp.int32)[None, :] < live_counts[:, None]
    ids = jnp.where(alive, block_index, cols).reshape(-1)

    place_here = jnp.stack([chip // SIDE, chip % SIDE])
    activations, table, part, meta_own, meta_oth, weight_term = layer(
        ids, own, oth, weight_matrix, adjacency_tiles, cotangent
    )
    rs_own, rs_oth = return_rows(place_here, meta_own, meta_oth, table, part)
    share = width // cols
    parts = lax.all_to_all(weight_term.reshape(cols, share, width), "col", 0, 0, tiled=True)
    parts, rs_oth = lax.optimization_barrier((parts, rs_oth))
    got = lax.ppermute(rs_oth, "col", swap)
    both = [
        (rs_own[d * SIDE : (d + 1) * SIDE].astype(F32) + got[d * SIDE : (d + 1) * SIDE].astype(F32))
        for d in range(SIDE)
    ]
    leaving = [b.astype(BF) for b in both[1:]]
    staying = both[0]
    along_x = staying
    for d in range(1, SIDE):
        along_x += lax.ppermute(leaving[d - 1], "col", shift(0, d)).astype(F32)
    summed = along_x[0]
    for d in range(1, SIDE):
        summed += lax.ppermute(along_x[d].astype(BF), "col", shift(d, 0)).astype(F32)
    projected_grad = summed.astype(BF)
    grad_features = dot(projected_grad, weight_matrix, 1, 1).astype(BF)

    weight_rows = jnp.sum(parts, axis=0)
    by_row = lax.all_to_all(
        jnp.broadcast_to(weight_rows[None], (zs,) + weight_rows.shape), "row", 0, 0, tiled=True
    )
    weight_rows = jnp.sum(by_row, axis=0) * total_rows ** (-0.5)
    by_col = lax.all_to_all(
        jnp.broadcast_to(weight_rows[None], (cols,) + weight_rows.shape), "col", 0, 0, tiled=True
    )
    return activations, grad_features, by_col.reshape(width, width)


def solution(mesh):
    return jax.shard_map(
        on_device,
        mesh=mesh,
        in_specs=(
            P(("row", "col"), None),
            P(("row", "col")),
            P(),
            P(("row", "col"), None),
            P(("row", "col")),
            P(("row", "col"), None, None, None),
            P(("row", "col"), None),
        ),
        out_specs=(P(("row", "col"), None), P(("row", "col"), None), P()),
        check_vma=False,
    )
```

```python
import functools

import jax
import jax.numpy as jnp
from jax import lax
from jax.experimental import pallas as pl
from jax.experimental.pallas import tpu as pltpu
from jax.sharding import PartitionSpec as P

BF = jnp.bfloat16
F32 = jnp.float32
META = 16
GROUP = 16
SIDE = 4
UNROLL = 16


def dot(a, b, ca=1, cb=0):
    return lax.dot_general(a, b, (((ca,), (cb,)), ((), ())), preferred_element_type=F32)


def one_hot(ids, count):
    rows = lax.broadcasted_iota(jnp.int32, (count, ids.shape[1]), 0).astype(F32)
    return jnp.where(rows == ids, 1.0, 0.0).astype(BF)


def layer_kernel(
    idx_ref,
    own_hbm,
    oth_hbm,
    w_ref,
    adj_hbm,
    cot_hbm,
    act_hbm,
    table_hbm,
    part_hbm,
    meta_own_hbm,
    meta_oth_hbm,
    gw,
    own_ref,
    oth_ref,
    table_ref,
    sent_ref,
    adj_ref,
    cot_ref,
    act_ref,
    slots,
    src,
    feats,
    part,
    row_sem,
    adj_sem,
    cot_sem,
    act_sem,
):
    chips, rows, width = own_ref.shape[0], own_ref.shape[1] - META, own_ref.shape[2]
    owners = 2 * chips
    cap = slots.shape[1] // owners
    blocks, nbr = adj_ref.shape[:2]
    groups = blocks // GROUP

    def fetch(g):
        at = pl.ds(g * GROUP, GROUP)
        band = pl.ds(g * GROUP * rows, GROUP * rows)
        return (
            pltpu.make_async_copy(adj_hbm.at[at], adj_ref.at[at], adj_sem.at[g]),
            pltpu.make_async_copy(cot_hbm.at[band], cot_ref.at[band], cot_sem.at[g]),
        )

    def flush(g):
        band = pl.ds(g * GROUP * rows, GROUP * rows)
        return pltpu.make_async_copy(act_ref.at[band], act_hbm.at[band], act_sem.at[g])

    take_own = pltpu.make_async_copy(own_hbm, own_ref, row_sem.at[0])
    take_oth = pltpu.make_async_copy(oth_hbm, oth_ref, row_sem.at[1])
    tail = pl.ds(rows, META)
    give_metas = (
        pltpu.make_async_copy(own_ref.at[:, tail], meta_own_hbm, row_sem.at[5]),
        pltpu.make_async_copy(oth_ref.at[:, tail], meta_oth_hbm, row_sem.at[6]),
    )
    give_table = pltpu.make_async_copy(table_ref, table_hbm, row_sem.at[2])

    def give_part(h):
        at = pl.ds(h * chips, chips)
        return pltpu.make_async_copy(sent_ref.at[at], part_hbm.at[at], row_sem.at[3 + h])

    take_own.start()
    take_oth.start()
    for g in range(groups):
        for copy in fetch(g):
            copy.start()

    part[...] = jnp.zeros_like(part)
    src[owners] = jnp.zeros(src.shape[1:], BF)

    for side, (ref, take) in enumerate(((own_ref, take_own), (oth_ref, take_oth))):
        take.wait()

        def spread_rows(i, carry):
            meta = ref[i, rows : rows + META, :].astype(F32)
            to_slot = one_hot(meta[0:1, :rows], owners * cap)
            to_place = one_hot(meta[0:1, rows : 2 * rows], rows)
            s = side * chips + i
            at = pl.ds(pl.multiple_of(s * cap, cap), cap)
            moved = dot(to_slot, ref[i, :rows, :])
            slots[:, at, :width] = moved.reshape(owners, cap, width)
            table = dot(to_slot, to_place, 1, 1)
            slots[:, at, width:] = table.reshape(owners, cap, rows)
            return carry

        lax.fori_loop(0, chips, spread_rows, 0, unroll=UNROLL)

    def place_rows(p, carry):
        table = slots[p, :, width:].astype(BF)
        table_ref[p] = table
        block = dot(table, slots[p, :, :width].astype(BF), 0, 0).astype(BF)
        feats[p] = block
        src[p] = dot(block, w_ref[...]).astype(BF)
        return carry

    lax.fori_loop(0, owners, place_rows, 0, unroll=UNROLL)
    give_table.start()
    for give in give_metas:
        give.start()

    def forward(b):
        ids = [idx_ref[b * nbr + j] for j in range(nbr)]
        tiles = [
            jnp.concatenate([adj_ref[b, 2 * q], adj_ref[b, 2 * q + 1]], axis=1)
            for q in range(nbr // 2)
        ]
        v = None
        for q in range(nbr // 2):
            picked = jnp.concatenate([src[ids[2 * q]], src[ids[2 * q + 1]]], axis=0)
            term = dot(tiles[q], picked)
            v = term if v is None else v + term
        return ids, tiles, v

    def middle(b, v):
        here = pl.ds(pl.multiple_of(b * rows, rows), rows)
        s = 1.0 / (1.0 + jnp.exp(-v))
        act_ref[here, :] = (v * s).astype(BF)
        slope = s * (1.0 + v * (1.0 - s))
        return (cot_ref[here, :].astype(F32) * slope).astype(BF)

    def backward(ids, tiles, grad):
        for q in range(nbr // 2):
            contrib = dot(tiles[q], grad, 0, 0)
            a, b = ids[2 * q], ids[2 * q + 1]
            old_a, old_b = part[a], part[b]
            part[a] = old_a + contrib[:rows]
            part[b] = old_b + contrib[rows:]

    def run_group(g, carry):
        for copy in fetch(g):
            copy.wait()
        ahead = forward(g * GROUP)
        for k in range(GROUP):
            grad = middle(g * GROUP + k, ahead[2])
            later = forward(g * GROUP + k + 1) if k + 1 < GROUP else None
            backward(ahead[0], ahead[1], grad)
            ahead = later
        flush(g).start()
        return carry

    lax.fori_loop(0, groups, run_group, 0)

    gw[...] = jnp.zeros_like(gw)

    def weight_term(p, carry):
        grad = part[p].astype(BF)
        sent_ref[p] = grad
        gw[...] += dot(feats[p], grad, 0, 0)
        return carry

    for h in range(2):
        lax.fori_loop(h * chips, (h + 1) * chips, weight_term, 0, unroll=UNROLL)
        give_part(h).start()

    for g in range(groups):
        flush(g).wait()
    give_table.wait()
    for give in give_metas:
        give.wait()
    for h in range(2):
        give_part(h).wait()


def return_kernel(
    me_ref,
    meta_own_hbm,
    meta_oth_hbm,
    table_hbm,
    part_hbm,
    rs_own_hbm,
    rs_oth_hbm,
    meta_own,
    meta_oth,
    table_ref,
    part_ref,
    rs_own_ref,
    rs_oth_ref,
    slots,
    meta_sem,
    part_sem,
    give_sem,
):
    chips, rows, width = rs_own_ref.shape
    owners = 2 * chips
    cap = slots.shape[1] // owners

    def take(h):
        at = pl.ds(h * chips, chips)
        return (
            pltpu.make_async_copy(table_hbm.at[at], table_ref.at[at], part_sem.at[2 * h]),
            pltpu.make_async_copy(part_hbm.at[at], part_ref.at[at], part_sem.at[2 * h + 1]),
        )

    metas = (
        pltpu.make_async_copy(meta_own_hbm, meta_own, meta_sem.at[0]),
        pltpu.make_async_copy(meta_oth_hbm, meta_oth, meta_sem.at[1]),
    )
    for copy in (*take(0), *take(1), *metas):
        copy.start()

    def to_slots(p, carry):
        slots[p] = dot(table_ref[p], part_ref[p])
        return carry

    for h in range(2):
        for copy in take(h):
            copy.wait()
        lax.fori_loop(h * chips, (h + 1) * chips, to_slots, 0, unroll=UNROLL)

    for copy in metas:
        copy.wait()
    my_y, my_x = me_ref[0], me_ref[1]
    gives = []
    for side, meta_ref, out, hbm in (
        (1, meta_oth, rs_oth_ref, rs_oth_hbm),
        (0, meta_own, rs_own_ref, rs_own_hbm),
    ):

        def collect_rows(i, carry):
            to_slot = one_hot(meta_ref[i].astype(F32)[0:1, :rows], owners * cap)
            s = side * chips + i
            at = pl.ds(pl.multiple_of(s * cap, cap), cap)
            held = slots[:, at, :].reshape(owners * cap, width).astype(BF)
            away_y = (i // SIDE + SIDE - my_y) % SIDE
            away_x = (i % SIDE + SIDE - my_x) % SIDE
            out[away_x * SIDE + away_y] = dot(to_slot, held, 0, 0).astype(BF)
            return carry

        lax.fori_loop(0, chips, collect_rows, 0, unroll=UNROLL)
        give = pltpu.make_async_copy(out, hbm, give_sem.at[side])
        give.start()
        gives.append(give)
    for give in gives:
        give.wait()


def return_rows(me, meta_own, meta_oth, table, part):
    chips, rows, width = part.shape[0] // 2, *part.shape[1:]
    owners = 2 * chips
    smem = pl.BlockSpec(memory_space=pltpu.SMEM)
    hbm = pl.BlockSpec(memory_space=pl.ANY)
    back = jax.ShapeDtypeStruct((chips, rows, width), BF)
    return pl.pallas_call(
        return_kernel,
        in_specs=[smem, hbm, hbm, hbm, hbm],
        out_specs=[hbm, hbm],
        out_shape=[back, back],
        scratch_shapes=[
            pltpu.VMEM((chips, META, width), BF),
            pltpu.VMEM((chips, META, width), BF),
            pltpu.VMEM(table.shape, BF),
            pltpu.VMEM(part.shape, BF),
            pltpu.VMEM(back.shape, BF),
            pltpu.VMEM(back.shape, BF),
            pltpu.VMEM((owners, table.shape[1], width), F32),
            pltpu.SemaphoreType.DMA((2,)),
            pltpu.SemaphoreType.DMA((4,)),
            pltpu.SemaphoreType.DMA((2,)),
        ],
        cost_estimate=pl.CostEstimate(
            flops=4 * owners * table.shape[1] * rows * width,
            bytes_accessed=12 * part.size,
            transcendentals=0,
        ),
        compiler_params=pltpu.CompilerParams(vmem_limit_bytes=58 * 1024 * 1024),
    )(me, meta_own, meta_oth, table, part)


def layer(ids, own, oth, w, adj, cot):
    chips, padded, width = own.shape
    rows = padded - META
    owners = 2 * chips
    blocks, nbr = adj.shape[:2]
    cap = 2 * rows // owners
    groups = blocks // GROUP
    vmem = pl.BlockSpec(memory_space=pltpu.VMEM)
    smem = pl.BlockSpec(memory_space=pltpu.SMEM)
    hbm = pl.BlockSpec(memory_space=pl.ANY)
    return pl.pallas_call(
        layer_kernel,
        in_specs=[smem, hbm, hbm, vmem, hbm, hbm],
        out_specs=[hbm, hbm, hbm, hbm, hbm, vmem],
        out_shape=[
            jax.ShapeDtypeStruct(cot.shape, BF),
            jax.ShapeDtypeStruct((owners, owners * cap, rows), BF),
            jax.ShapeDtypeStruct((owners, rows, width), BF),
            jax.ShapeDtypeStruct((chips, META, width), BF),
            jax.ShapeDtypeStruct((chips, META, width), BF),
            jax.ShapeDtypeStruct((width, width), F32),
        ],
        scratch_shapes=[
            pltpu.VMEM(own.shape, BF),
            pltpu.VMEM(own.shape, BF),
            pltpu.VMEM((owners, owners * cap, rows), BF),
            pltpu.VMEM((owners, rows, width), BF),
            pltpu.VMEM(adj.shape, BF),
            pltpu.VMEM(cot.shape, BF),
            pltpu.VMEM(cot.shape, BF),
            pltpu.VMEM((owners, owners * cap, width + rows), F32),
            pltpu.VMEM((owners + 1, rows, width), BF),
            pltpu.VMEM((owners, rows, width), BF),
            pltpu.VMEM((owners + 1, rows, width), F32),
            pltpu.SemaphoreType.DMA((7,)),
            pltpu.SemaphoreType.DMA((groups,)),
            pltpu.SemaphoreType.DMA((groups,)),
            pltpu.SemaphoreType.DMA((groups,)),
        ],
        compiler_params=pltpu.CompilerParams(vmem_limit_bytes=50 * 1024 * 1024),
    )(ids, own, oth, w, adj, cot)


def on_device(
    node_features,
    reorder_target,
    weight_matrix,
    block_index,
    live_counts,
    adjacency_tiles,
    cotangent,
):
    cols = lax.axis_size("col")
    zs = lax.axis_size("row")
    chips = cols // 2
    rows, width = node_features.shape
    total_rows = rows * cols * zs
    nbr = adjacency_tiles.shape[1]
    swap = [(i, i ^ 1) for i in range(cols)]
    same_core = [[2 * i + c for i in range(chips)] for c in range(2)]
    chip = lax.axis_index("col") // 2

    def shift(dy, dx):
        pairs = []
        for i in range(cols):
            y, x, c = i // (2 * SIDE), i // 2 % SIDE, i % 2
            pairs.append((i, ((y + dy) % SIDE * SIDE + (x + dx) % SIDE) * 2 + c))
        return pairs


    owner = reorder_target // rows
    place = reorder_target % rows
    earlier = jnp.arange(rows)[:, None] < jnp.arange(rows)[None, :]
    rank = jnp.sum((owner[:, None] == owner[None, :]) & earlier, axis=0, dtype=jnp.int32)
    cap = 2 * rows // cols
    meta = jnp.concatenate([owner * cap + rank, place]).astype(BF)[None, :]
    block = jnp.concatenate([node_features, jnp.broadcast_to(meta, (META, width))], axis=0)
    own = lax.all_to_all(
        jnp.broadcast_to(block[None], (chips,) + block.shape),
        "col",
        0,
        0,
        tiled=True,
        axis_index_groups=same_core,
    )
    oth = lax.ppermute(own, "col", swap)
    alive = jnp.arange(nbr, dtype=jnp.int32)[None, :] < live_counts[:, None]
    ids = jnp.where(alive, block_index, cols).reshape(-1)

    place_here = jnp.stack([chip // SIDE, chip % SIDE])
    activations, table, part, meta_own, meta_oth, weight_term = layer(
        ids, own, oth, weight_matrix, adjacency_tiles, cotangent
    )
    rs_own, rs_oth = return_rows(place_here, meta_own, meta_oth, table, part)
    share = width // cols
    parts = lax.all_to_all(weight_term.reshape(cols, share, width), "col", 0, 0, tiled=True)
    parts, rs_oth = lax.optimization_barrier((parts, rs_oth))
    got = lax.ppermute(rs_oth, "col", swap)
    both = [
        (rs_own[d * SIDE : (d + 1) * SIDE].astype(F32) + got[d * SIDE : (d + 1) * SIDE].astype(F32))
        for d in range(SIDE)
    ]
    leaving = [b.astype(BF) for b in both[1:]]
    staying = both[0]
    along_x = staying
    for d in range(1, SIDE):
        along_x += lax.ppermute(leaving[d - 1], "col", shift(0, d)).astype(F32)
    summed = along_x[0]
    for d in range(1, SIDE):
        summed += lax.ppermute(along_x[d].astype(BF), "col", shift(d, 0)).astype(F32)
    projected_grad = summed.astype(BF)
    grad_features = dot(projected_grad, weight_matrix, 1, 1).astype(BF)

    weight_rows = jnp.sum(parts, axis=0)
    by_row = lax.all_to_all(
        jnp.broadcast_to(weight_rows[None], (zs,) + weight_rows.shape), "row", 0, 0, tiled=True
    )
    weight_rows = jnp.sum(by_row, axis=0) * total_rows ** (-0.5)
    by_col = lax.all_to_all(
        jnp.broadcast_to(weight_rows[None], (cols,) + weight_rows.shape), "col", 0, 0, tiled=True
    )
    return activations, grad_features, by_col.reshape(width, width)


def solution(mesh):
    return jax.shard_map(
        on_device,
        mesh=mesh,
        in_specs=(
            P(("row", "col"), None),
            P(("row", "col")),
            P(),
            P(("row", "col"), None),
            P(("row", "col")),
            P(("row", "col"), None, None, None),
            P(("row", "col"), None),
        ),
        out_specs=(P(("row", "col"), None), P(("row", "col"), None), P()),
        check_vma=False,
    )
```
